32 devices in a mesh: group: 2 (over y), seq: 4 (over z), head: 4 (over x, core), pair: 1.
Axes of the slice: x: 2, y: 2, z: 4, core: 2. Of those that a mesh axis runs over, the one named last changes fastest.
Arguments:
- query_states: bfloat16 [2048, 4096], P(('group', 'seq'), ('head', 'pair')), parts along dimension 0, may hold values from -6 to 6
- key_states: bfloat16 [2048, 512], P(('group', 'seq'), 'head'), parts along dimension 0, may hold values from -6 to 6
- value_states: bfloat16 [2048, 512], P(('group', 'seq'), 'head'), parts along dimension 0, may hold values from -12 to 12
- sink_logits: float32 [64], P(('head', 'pair')), may hold values from 0 to 5
- segment_ids: int32 [2048], P('group'), parts along dimension 0, may hold values from 0 to 11, never falling along the last dimension, each value on 1 to 256 neighbouring positions
- residual: bfloat16 [2048, 1536], P(('group', 'seq', 'head', 'pair')), parts along dimension 0, may hold values from -6 to 6
- out_weight: bfloat16 [4096, 1536], P(('head', 'pair')), may hold values from -0.09375 to 0.09375
- norm_gain: float32 [1536], replicated, may hold values from 0.5 to 1.5
- expert_ids: int32 [2048, 4], P(('group', 'seq', 'head', 'pair')), parts along dimension 0, may hold values from 0 to 7, all different within a row; in each aligned block of 64 rows (0 to 63, 64 to 127, ...) at most 48 rows name the same one
- route_weights: float32 [2048, 4], P(('group', 'seq', 'head', 'pair')), parts along dimension 0, may hold values from 0.1 to 1
- gate_proj: bfloat16 [16, 1536, 768], P(('seq', 'head'), None, 'pair'), may hold values from -0.15625 to 0.15625
- up_proj: bfloat16 [16, 1536, 768], P(('seq', 'head'), None, 'pair'), may hold values from -0.15625 to 0.15625
- down_proj: bfloat16 [16, 768, 1536], P(('seq', 'head'), 'pair'), may hold values from -0.15625 to 0.15625
Outputs:
- layer_out: bfloat16 [2048, 1536], P(('group', 'seq', 'head', 'pair')), parts along dimension 0
The draws below stay inside these ranges and needn't reach their ends.
There are 2 independent parts, one for each index of `group`. The reference program is written for one: setup_inputs(seed, part) draws one part's arguments, and reference() takes and returns one part's arrays. A program takes and returns all parts, laid end to end along the dimension named above; an argument that names none is the same for every part. Nothing has to cross between parts.
Inputs may be any that keep to these rules, and one draw needn't show every extreme that they name: `segment_ids`: never falling along the sequence; each passage holds 1 to 256 tokens and one holds exactly 256. `expert_ids`: each row names 4 different experts. Among the rows of one device (aligned blocks of 64 rows) no expert is named by more than 48 rows, a bound that some block reaches.
All inputs are finite; a program needn't handle non-finite values.
Results may differ from the reference program's by a relative error of at most 0.015.
Values may be sent and summed in bfloat16 or wider, within the bound.
A program may use at most 64 MiB of HBM per device.

```python
import math
import jax
import jax.numpy as jnp
import numpy as np
from jax import lax

D = 1536
FF = 1536
HEADS = 64
KV_HEADS = 8
HEAD_DIM = 64
TOP = 4
WINDOW = 128
TOK_DEV = 256
TOKENS = 1024
TOK_SHARD = 64
HEAD_BLOCK = 16
EXPERTS = 8
EXPERT_HALVES = 16
FF_HALF = 768
FF_QUARTER = 384
CAP = 48
SEGMENTS = 12


def draw_query_states(key, part):
    shape = (TOKENS, HEADS * HEAD_DIM)
    result = jnp.clip(jax.random.normal(jax.random.fold_in(key, 12), shape), -6.0, 6.0)
    return result.astype(jnp.bfloat16)


def draw_key_states(key, part):
    shape = (TOKENS, KV_HEADS * HEAD_DIM)
    result = jnp.clip(jax.random.normal(jax.random.fold_in(key, 22), shape), -6.0, 6.0)
    return result.astype(jnp.bfloat16)


def block_scale(rng, shape, split, least, top_value):
    factor_of, own = 1.0, jax.random.fold_in(rng, 6)
    for axis_at, shards_of in split:
        steps = jnp.exp(jax.random.uniform(jax.random.fold_in(own, axis_at), (shards_of,), jnp.float32, least / len(split), top_value / len(split)))
        factor_of = factor_of * jnp.repeat(steps, shape[axis_at] // shards_of).reshape([-1 if axis == axis_at else 1 for axis in range(len(shape))])
    return factor_of


def length_profile(amount, total, reach, lean):
    portions = [(1 << 20) // math.isqrt(grade ** lean) + 1 for grade in range(2, amount + 1)]
    spare, holding = total - reach - (amount - 1), [1] * (amount - 1)
    while spare > 0:
        movable = [i for i in range(amount - 1) if holding[i] < reach]
        pool, remaining = sum([portions[i] for i in movable]), spare
        for i in movable:
            addition = min(reach - holding[i], max(1, remaining * portions[i] // pool), spare)
            holding[i] = holding[i] + addition
            spare = spare - addition
    return np.array([reach] + holding)


def uneven_parts(rng, amount, total, limit, lean):
    if amount == 2:
        one = jax.random.randint(rng, (), max(1, total - limit), min(limit, total - 1) + 1)
        return jnp.stack([one, total - one])
    lengths = jnp.asarray(length_profile(amount, total, limit, lean), jnp.int32)
    twos = (amount - 1) // 2
    source_of, receiver = lengths[1:1 + 2 * twos:2], lengths[2:2 + 2 * twos:2]
    margin = jnp.minimum(source_of - 1, limit - receiver)
    moved = jax.random.randint(jax.random.fold_in(rng, 1), (twos,), 0, 1 << 20) % (margin + 1)
    lengths = lengths.at[1:1 + 2 * twos:2].set(source_of - moved).at[2:2 + 2 * twos:2].set(receiver + moved)
    return lengths[jax.random.permutation(jax.random.fold_in(rng, 2), amount)]


def shared_out(own_key, own, number, rows, amount, top, most, lean):
    order = jax.random.permutation(own_key, amount)
    packed, common = load_shares(amount, rows * top, most, lean, True), load_shares(amount, rows * top, most, lean, False)
    places = jnp.arange(amount)

    def named(lengths, turn):
        used = int((lengths > 0).sum())
        fixed = max(1, used // 4)
        moved = fixed + (places - fixed + turn * (used - fixed)) % max(1, amount - fixed)
        return jnp.zeros((amount,), jnp.int32).at[order[jnp.where(places < fixed, places, moved)]].set(jnp.asarray(lengths, jnp.int32))

    lengths = jnp.where(number % 4 == 0, named(packed, number // 4), named(common, number - number // 4 - 1))
    mixed = jax.random.permutation(jax.random.fold_in(own, 3), amount)
    giver, sink = mixed[0:amount // 2 * 2:2], mixed[1:amount // 2 * 2:2]
    margin = jnp.minimum(lengths[giver] - 1, most - lengths[sink]) // 2
    margin = jnp.where((giver == order[0]) | (sink == order[0]) | (lengths[sink] == 0), 0, jnp.maximum(margin, 0))
    moved = jax.random.randint(jax.random.fold_in(own, 4), (amount // 2,), 0, 1 << 20) % (margin + 1)
    lengths = lengths.at[giver].add(-moved).at[sink].add(moved)
    members = jnp.searchsorted(jnp.cumsum(lengths), jnp.arange(rows * top), side="right").astype(jnp.int32)
    table = members.reshape(top, rows).T
    table = table[jax.random.permutation(jax.random.fold_in(own, 1), rows)]
    turn = jax.random.randint(jax.random.fold_in(own, 2), (rows, 1), 0, top)
    return jnp.take_along_axis(table, (jnp.arange(top)[None, :] + turn) % top, axis=1)


def load_shares(number_of, total, most, skew, full):
    portions = [(1 << 20) // math.isqrt(grade ** skew) + 1 for grade in range(1, number_of + 1)]
    largest = most if full else min(most, max(-(-total // number_of), total * portions[0] // sum(portions)))
    least = 1 if total - largest >= number_of - 1 else 0
    given, spare = [largest] + [least] * (number_of - 1), total - largest - least * (number_of - 1)
    while spare > 0:
        movable = [i for i in range(1, number_of) if given[i] < largest] or [i for i in range(1, number_of) if given[i] < most]
        mass, budget = sum([portions[i] for i in movable]), spare
        for i in movable:
            extra = min(most - given[i], max(1, budget * portions[i] // mass), spare)
            given[i] = given[i] + extra
            spare = spare - extra
    return np.array(given)


def normal_values(own_key, dims, spread, most, pieces=(), kind=jnp.bfloat16):
    drawn = spread * jax.random.normal(own_key, dims, jnp.float32)
    if pieces:
        drawn = drawn * block_scale(own_key, dims, pieces, -0.22, 0.18)
    return jnp.clip(drawn, -most, most).astype(kind)


def setup_inputs(seed: int = 0, part: int = 0) -> dict:
    arg_keys = jax.random.split(jax.random.key(seed), 14)
    own_keys = jax.random.split(jax.random.fold_in(arg_keys[13], part), 14)
    query_states = draw_query_states(jax.random.fold_in(jax.random.fold_in(arg_keys[13], part), 71), part)
    key_states = draw_key_states(jax.random.fold_in(jax.random.fold_in(arg_keys[13], part), 71), part)
    value_states = normal_values(own_keys[2], (TOKENS, KV_HEADS * HEAD_DIM), 2.0, 12.0, ((0, 4), (1, 4)))
    sink_logits = jnp.clip(5.0 * jax.random.uniform(arg_keys[3], (HEADS,), jnp.float32) ** block_scale(arg_keys[3], (HEADS,), ((0, 4),), -0.2, 0.2), 0.0, 5.0)
    segment_ids = jnp.searchsorted(jnp.cumsum(uneven_parts(own_keys[4], SEGMENTS, TOKENS, TOK_DEV, 1)), jnp.arange(TOKENS), side="right").astype(jnp.int32)
    residual = normal_values(own_keys[5], (TOKENS, D), 1.0, 6.0, ((0, 16),))
    out_weight = normal_values(arg_keys[6], (HEADS * HEAD_DIM, D), (HEADS * HEAD_DIM) ** -0.5, 0.09375, ((0, 4),))
    norm_gain = jnp.clip(1.0 + 0.1 * jax.random.normal(arg_keys[7], (D,), jnp.float32), 0.5, 1.5)
    expert_ids_keys = jax.random.split(jax.random.fold_in(own_keys[8], 1), TOKENS // TOK_SHARD)
    expert_ids_turns = jax.random.permutation(jax.random.fold_in(own_keys[8], 3), TOKENS // TOK_SHARD)
    expert_ids = jax.vmap(lambda own, number: shared_out(jax.random.fold_in(own_keys[8], 2), own, number, TOK_SHARD, EXPERTS, TOP, CAP, 2))(expert_ids_keys, expert_ids_turns).reshape((TOKENS, TOP))
    route_weights = jnp.clip(jnp.exp(math.log(1.0) - 2.3025851 * jax.random.uniform(own_keys[9], (TOKENS, TOP), jnp.float32) ** block_scale(own_keys[9], (TOKENS, TOP), ((0, 16),), -0.2, 0.2)), 0.1, 1.0)
    gate_proj = normal_values(arg_keys[10], (EXPERT_HALVES, D, FF_HALF), D ** -0.5, 0.15625, ((0, 16),))
    up_proj = normal_values(arg_keys[11], (EXPERT_HALVES, D, FF_HALF), D ** -0.5, 0.15625, ((0, 16),))
    down_proj = normal_values(arg_keys[12], (EXPERT_HALVES, FF_HALF, D), FF ** -0.5, 0.15625, ((0, 16),))
    return {"query_states": query_states, "key_states": key_states, "value_states": value_states, "sink_logits": sink_logits, "segment_ids": segment_ids, "residual": residual, "out_weight": out_weight, "norm_gain": norm_gain, "expert_ids": expert_ids, "route_weights": route_weights, "gate_proj": gate_proj, "up_proj": up_proj, "down_proj": down_proj}


def round_keep(values):
    return lax.optimization_barrier(values.astype(jnp.bfloat16)).astype(jnp.float32)

def attention(query_states, key_states, value_states, sink_logits, segment_ids):
    group_size = HEADS // KV_HEADS
    block_rows = min(512, TOK_DEV)
    key_padded = jnp.concatenate([jnp.zeros((WINDOW, KV_HEADS * HEAD_DIM), jnp.bfloat16), key_states], 0)
    value_padded = jnp.concatenate([jnp.zeros((WINDOW, KV_HEADS * HEAD_DIM), jnp.bfloat16), value_states], 0)
    seg_padded = jnp.concatenate([jnp.full((WINDOW,), -1, jnp.int32), segment_ids.astype(jnp.int32)], 0)

    def attend(block_index):
        first_row = block_index * block_rows
        query_block = lax.dynamic_slice_in_dim(query_states, first_row, block_rows, 0).astype(jnp.float32)
        query_block = query_block.reshape(block_rows, HEADS, HEAD_DIM)
        key_block = lax.dynamic_slice_in_dim(key_padded, first_row, block_rows + WINDOW, 0).astype(jnp.float32)
        key_block = jnp.repeat(key_block.reshape(block_rows + WINDOW, KV_HEADS, HEAD_DIM), group_size, axis=1)
        value_block = lax.dynamic_slice_in_dim(value_padded, first_row, block_rows + WINDOW, 0).astype(jnp.float32)
        value_block = jnp.repeat(value_block.reshape(block_rows + WINDOW, KV_HEADS, HEAD_DIM), group_size, axis=1)
        query_pos = first_row + jnp.arange(block_rows, dtype=jnp.int32)
        key_pos = first_row - WINDOW + jnp.arange(block_rows + WINDOW, dtype=jnp.int32)
        query_seg = lax.dynamic_slice_in_dim(segment_ids.astype(jnp.int32), first_row, block_rows, 0)
        key_seg = lax.dynamic_slice_in_dim(seg_padded, first_row, block_rows + WINDOW, 0)
        scores = jnp.einsum('qhd,khd->hqk', query_block, key_block) * HEAD_DIM ** (-0.5)
        visible = (key_pos[None, :] <= query_pos[:, None]) & (query_pos[:, None] - key_pos[None, :] < WINDOW)
        visible = visible & (key_pos[None, :] >= 0) & (key_seg[None, :] == query_seg[:, None])
        masked = jnp.where(visible[None], scores, -1e+30)
        row_max = jnp.maximum(lax.optimization_barrier(jnp.max(masked, -1)), sink_logits[:, None])
        weights_exp = jnp.exp(masked - row_max[..., None])
        denominator = lax.optimization_barrier(jnp.sum(weights_exp, -1)) + jnp.exp(sink_logits[:, None] - row_max)
        probs = (weights_exp / denominator[..., None]).astype(jnp.bfloat16)
        attended = jnp.einsum('hqk,khd->qhd', probs.astype(jnp.float32), value_block)
        return attended.astype(jnp.bfloat16).reshape(block_rows, HEADS * HEAD_DIM)
    blocks = lax.map(attend, jnp.arange(TOKENS // block_rows, dtype=jnp.int32))
    return blocks.reshape(TOKENS, HEADS * HEAD_DIM)

def reference(query_states, key_states, value_states, sink_logits, segment_ids, residual, out_weight, norm_gain, expert_ids, route_weights, gate_proj, up_proj, down_proj):
    attended = attention(query_states, key_states, value_states, sink_logits, segment_ids)
    width_block = HEAD_BLOCK * HEAD_DIM
    hidden_state = residual.astype(jnp.float32)
    for block_index in range(HEADS // HEAD_BLOCK):
        columns = attended[:, block_index * width_block:(block_index + 1) * width_block]
        rows_w = out_weight[block_index * width_block:(block_index + 1) * width_block]
        hidden_state = hidden_state + round_keep(jnp.dot(columns, rows_w, preferred_element_type=jnp.float32))
    variance = lax.optimization_barrier(jnp.mean(hidden_state * hidden_state, -1, keepdims=True))
    normed = (hidden_state * lax.rsqrt(variance + 1e-05) * norm_gain).astype(jnp.bfloat16)
    sources = TOKENS // TOK_SHARD
    assigned = TOK_SHARD * TOP
    slot_rows = sources * CAP
    id_blocks = expert_ids.astype(jnp.int32).reshape(sources, assigned)
    onehot = (id_blocks[..., None] == jnp.arange(EXPERTS, dtype=jnp.int32)).astype(jnp.int32)
    before = jnp.cumsum(onehot, axis=1, dtype=jnp.int32) - onehot
    slot_rank = lax.optimization_barrier(jnp.sum(before * onehot, -1)).astype(jnp.int32)
    source_index = jnp.arange(sources, dtype=jnp.int32)[:, None]
    slot_index = id_blocks * slot_rows + source_index * CAP + slot_rank
    token_index = source_index * TOK_SHARD + jnp.arange(assigned, dtype=jnp.int32)[None, :] // TOP
    token_table = jnp.zeros((EXPERTS * slot_rows,), jnp.int32).at[slot_index.reshape(-1)].set(token_index.reshape(-1))
    weight_table = jnp.zeros((EXPERTS * slot_rows,), jnp.float32).at[slot_index.reshape(-1)].set(route_weights.reshape(-1))
    token_table = token_table.reshape(EXPERTS, slot_rows)
    weight_table = weight_table.reshape(EXPERTS, slot_rows)
    gate_four = gate_proj.reshape(EXPERTS, 2, D, FF_HALF)
    up_four = up_proj.reshape(EXPERTS, 2, D, FF_HALF)
    down_four = down_proj.reshape(EXPERTS, 2, FF_HALF, D)

    def one_expert(totals, inputs):
        gate_e, up_e, down_e, tokens_e, weights_e = inputs
        rows = jnp.take(normed, tokens_e, axis=0)
        expert_out = jnp.zeros((slot_rows, D), jnp.float32)
        for half_idx in range(2):
            gate_val = jnp.minimum(jnp.dot(rows, gate_e[half_idx], preferred_element_type=jnp.float32), 7.0)
            up_val = jnp.clip(jnp.dot(rows, up_e[half_idx], preferred_element_type=jnp.float32), -7.0, 7.0)
            activated = ((up_val + 1.0) * gate_val * jax.nn.sigmoid(1.702 * gate_val)).astype(jnp.bfloat16)
            for quarter_idx in range(2):
                low = quarter_idx * FF_QUARTER
                partial_value = jnp.dot(activated[:, low:low + FF_QUARTER], down_e[half_idx][low:low + FF_QUARTER], preferred_element_type=jnp.float32)
                expert_out = expert_out + round_keep(partial_value)
        totals = totals.at[tokens_e].add(weights_e[:, None] * expert_out)
        return (totals, None)
    mixture, unused = lax.scan(one_expert, jnp.zeros((TOKENS, D), jnp.float32), (gate_four, up_four, down_four, token_table, weight_table))
    return (hidden_state + mixture).astype(jnp.bfloat16)
```

```python
import functools

import jax
import jax.numpy as jnp
from jax import lax
from jax.experimental import pallas as pl
from jax.experimental.pallas import tpu as pltpu
from jax.sharding import PartitionSpec as P

HEADS = 64
KV_HEADS = 8
HEAD_DIM = 64
WINDOW = 128


def passed_along(value, axis, by):
    peers = lax.axis_size(axis)
    pairs = [(i, i + by) for i in range(peers) if 0 <= i + by < peers]
    return lax.ppermute(value, axis, pairs)


def partner(value, axis, distance):
    return lax.ppermute(value, axis, [(i, i ^ 1 << distance) for i in range(lax.axis_size(axis))])


def round_keep(values):
    return lax.optimization_barrier(values.astype(jnp.bfloat16)).astype(jnp.float32)


def window_attention(
    query_block, key_block, value_block, query_pos, key_pos, query_seg, key_seg, sink_logits
):
    scores = jnp.einsum(
        "qhd,khd->hqk", query_block, key_block, preferred_element_type=jnp.float32
    ) * HEAD_DIM ** (-0.5)
    visible = (key_pos[None, :] <= query_pos[:, None]) & (
        query_pos[:, None] - key_pos[None, :] < WINDOW
    )
    visible = visible & (key_pos[None, :] >= 0) & (key_seg[None, :] == query_seg[:, None])
    masked = jnp.where(visible[None], scores, -1e30)
    row_max = jnp.maximum(jnp.max(masked, -1), sink_logits[:, None])
    weights_exp = jnp.exp(masked - row_max[..., None])
    denominator = jnp.sum(weights_exp, -1) + jnp.exp(sink_logits[:, None] - row_max)
    probs = (weights_exp / denominator[..., None]).astype(jnp.bfloat16)
    attended = jnp.einsum("hqk,khd->qhd", probs, value_block, preferred_element_type=jnp.float32)
    return attended.astype(jnp.bfloat16)


def per_device(
    query_states,
    key_states,
    value_states,
    sink_logits,
    segment_ids,
    residual,
    out_weight,
    norm_gain,
    expert_ids,
    route_weights,
    gate_proj,
    up_proj,
    down_proj,
):
    tok_rows = query_states.shape[0]
    local_heads = query_states.shape[1] // HEAD_DIM
    local_groups = key_states.shape[1] // HEAD_DIM
    group_size = HEADS // KV_HEADS
    tail_keys, tail_values = passed_along(
        (key_states[tok_rows - WINDOW :], value_states[tok_rows - WINDOW :]), "seq", 1
    )
    ext_keys = jnp.concatenate([tail_keys, key_states], 0).reshape(
        tok_rows + WINDOW, local_groups, HEAD_DIM
    )
    ext_values = jnp.concatenate([tail_values, value_states], 0).reshape(
        tok_rows + WINDOW, local_groups, HEAD_DIM
    )
    kv_owner = (
        lax.axis_index("pair") * local_heads + jnp.arange(local_heads, dtype=jnp.int32)
    ) // group_size
    head_select = (kv_owner[:, None] == jnp.arange(local_groups, dtype=jnp.int32)[None, :]).astype(
        jnp.bfloat16
    )
    keys_per_head = jnp.einsum(
        "kcd,hc->khd", ext_keys, head_select, preferred_element_type=jnp.float32
    ).astype(jnp.bfloat16)
    values_per_head = jnp.einsum(
        "kcd,hc->khd", ext_values, head_select, preferred_element_type=jnp.float32
    ).astype(jnp.bfloat16)
    query_heads = query_states.reshape(tok_rows, local_heads, HEAD_DIM)
    seq_start = lax.axis_index("seq") * tok_rows
    seg_padded = jnp.concatenate([jnp.full((WINDOW,), -1, jnp.int32), segment_ids], 0)
    block_rows = min(512, tok_rows)

    def attend(block_index):
        first_row = block_index * block_rows
        query_pos = seq_start + first_row + jnp.arange(block_rows, dtype=jnp.int32)
        key_pos = seq_start + first_row - WINDOW + jnp.arange(block_rows + WINDOW, dtype=jnp.int32)
        query_seg = lax.dynamic_slice_in_dim(segment_ids, seq_start + first_row, block_rows, 0)
        key_seg = lax.dynamic_slice_in_dim(
            seg_padded, seq_start + first_row, block_rows + WINDOW, 0
        )
        return window_attention(
            query_heads,
            keys_per_head,
            values_per_head,
            query_pos,
            key_pos,
            query_seg,
            key_seg,
            sink_logits,
        )

    attended = lax.map(attend, jnp.arange(tok_rows // block_rows, dtype=jnp.int32))
    attended = attended.reshape(tok_rows, local_heads * HEAD_DIM)
    shard_rows = residual.shape[0]
    width = residual.shape[1]
    projected = lax.psum_scatter(
        round_keep(jnp.dot(attended, out_weight, preferred_element_type=jnp.float32)).astype(
            jnp.bfloat16
        ),
        ("head", "pair"),
        scatter_dimension=0,
        tiled=True,
    ).astype(jnp.float32)
    hidden_state = residual.astype(jnp.float32) + projected
    variance = jnp.mean(hidden_state * hidden_state, -1, keepdims=True)
    normed = (hidden_state * lax.rsqrt(variance + 1e-05) * norm_gain).astype(jnp.bfloat16)
    top_count = expert_ids.shape[1]
    experts = lax.axis_size("seq") * lax.axis_size("head") // 2
    capacity = min(shard_rows, max(2, 3 * shard_rows * top_count // (2 * experts)))
    flat_ids = expert_ids.reshape(-1)
    onehot = (flat_ids[:, None] == jnp.arange(experts, dtype=jnp.int32)[None, :]).astype(jnp.int32)
    places = jnp.arange(flat_ids.shape[0], dtype=jnp.int32)
    earlier = (places[None, :] < places[:, None]).astype(jnp.bfloat16)
    before = jnp.dot(
        earlier, onehot.astype(jnp.bfloat16), preferred_element_type=jnp.float32
    ).astype(jnp.int32)
    slot_rank = jnp.sum(before * onehot, -1)
    slot_index = flat_ids * capacity + slot_rank
    dispatch_mat = (
        slot_index[None, :] == jnp.arange(experts * capacity, dtype=jnp.int32)[:, None]
    ).astype(jnp.bfloat16)
    repeated = jnp.repeat(normed, top_count, axis=0)
    outgoing = jnp.dot(dispatch_mat, repeated, preferred_element_type=jnp.float32).astype(
        jnp.bfloat16
    )
    outgoing = outgoing.reshape(experts, capacity, width)
    half_idx = lax.axis_index("head") % 2
    half_width = width // 2
    split_rows = outgoing.reshape(experts, capacity, 2, half_width).transpose(0, 2, 1, 3)
    split_rows = split_rows.reshape(2 * experts, capacity, half_width)
    own_half = lax.all_to_all(split_rows, ("seq", "head"), split_axis=0, concat_axis=0, tiled=True)
    other_half = partner(own_half, "head", 0)
    arrived = jnp.where(
        half_idx == 0,
        jnp.concatenate([own_half, other_half], -1),
        jnp.concatenate([other_half, own_half], -1),
    )
    gate_local = gate_proj[0]
    up_local = up_proj[0]
    down_local = down_proj[0]
    piece_rows = lax.all_gather(arrived, "pair", axis=0, tiled=True)
    flat_rows = piece_rows.reshape(-1, width)
    gate_val = jnp.minimum(jnp.dot(flat_rows, gate_local, preferred_element_type=jnp.float32), 7.0)
    up_val = jnp.clip(jnp.dot(flat_rows, up_local, preferred_element_type=jnp.float32), -7.0, 7.0)
    activated = ((up_val + 1.0) * gate_val * jax.nn.sigmoid(1.702 * gate_val)).astype(jnp.bfloat16)
    partial_value = round_keep(jnp.dot(activated, down_local, preferred_element_type=jnp.float32))
    quarter_terms = partial_value.reshape(piece_rows.shape)
    pair_sums = lax.psum_scatter(
        quarter_terms.astype(jnp.bfloat16), "pair", scatter_dimension=0, tiled=True
    ).astype(jnp.float32)
    kept_half = lax.dynamic_slice_in_dim(pair_sums, half_idx * half_width, half_width, 2)
    given_half = lax.dynamic_slice_in_dim(pair_sums, (1 - half_idx) * half_width, half_width, 2)
    partner_half = partner(given_half.astype(jnp.bfloat16), "head", 0).astype(given_half.dtype)
    merged = kept_half + partner_half
    returned = lax.all_to_all(
        merged.astype(jnp.bfloat16), ("seq", "head"), split_axis=0, concat_axis=0, tiled=True
    ).astype(merged.dtype)
    expert_out = (
        returned.reshape(experts, 2, capacity, half_width)
        .transpose(0, 2, 1, 3)
        .reshape(experts, capacity, width)
    )
    slot_table = slot_index.reshape(shard_rows, top_count)
    columns_all = jnp.arange(experts * capacity, dtype=jnp.int32)
    combine_mat = jnp.sum(
        jnp.where(
            slot_table[:, :, None] == columns_all[None, None, :], route_weights[:, :, None], 0.0
        ),
        axis=1,
    )
    mixture = jnp.dot(
        combine_mat, expert_out.reshape(experts * capacity, width), precision=lax.Precision.HIGHEST
    )
    return (hidden_state + mixture).astype(jnp.bfloat16)


BF16, F32 = jnp.bfloat16, jnp.float32
MESH = pl.DeviceIdType.MESH
LANES = 128


def pick(table, index):
    result = jnp.int32(table[0])
    for i in range(1, len(table)):
        result = jnp.where(index == i, jnp.int32(table[i]), result)
    return result


def as_column(row, dtype=F32):
    n = row.shape[1]
    at = lax.broadcasted_iota(jnp.int32, (n, n), 0) == lax.broadcasted_iota(jnp.int32, (n, n), 1)
    return jnp.sum(jnp.where(at, row.astype(F32), 0.0), 1, keepdims=True)


def layer_kernel(
    planes, experts,
    q_ref, k_ref, v_ref, sink_ref, seg_ref, res_ref, wo_hbm, gain_ref, ids_ref, rw_ref,
    gate_hbm, up_hbm, down_hbm,
    out_ref,
    wo, gate, up, down, tail_k, tail_v, ext, kk, vv, attended, proj, proj_core, proj_x, proj_got,
    hidden, xbuf, act, obuf, rc, s_out, rx, s_own, rz,
    w_sem, halo_send, halo_recv, pc_send, pc_recv, px_send, px_recv,
    gz_send, gz_recv, gx_send, gx_recv, gc_send, gc_recv,
    rc_send, rc_recv, rx_send, rx_recv, rz_send, rz_recv,
):
    z, head = lax.axis_index("seq"), lax.axis_index("head")
    x, core = head // 2, head % 2
    other_core = {"seq": z, "head": x * 2 + 1 - core}
    other_x = {"seq": z, "head": (1 - x) * 2 + core}
    rows, width = res_ref.shape
    ff = gate.shape[1]

    def remote(src, dst, send, recv, to):
        return pltpu.make_async_remote_copy(
            src_ref=src, dst_ref=dst, send_sem=send, recv_sem=recv, device_id=to, device_id_type=MESH
        )

    loads = [
        pltpu.make_async_copy(wo_hbm, wo, w_sem.at[0]),
        pltpu.make_async_copy(gate_hbm.at[0], gate, w_sem.at[1]),
        pltpu.make_async_copy(up_hbm.at[0], up, w_sem.at[2]),
        pltpu.make_async_copy(down_hbm.at[0], down, w_sem.at[3]),
    ]
    for load in loads:
        load.start()

    barrier = pltpu.get_barrier_semaphore()
    pl.semaphore_signal(barrier, inc=1, device_id=other_core, device_id_type=MESH)
    pl.semaphore_signal(barrier, inc=1, device_id=other_x, device_id_type=MESH)
    for far in range(1, planes):
        to = {"seq": lax.rem(z + far, planes), "head": head}
        pl.semaphore_signal(barrier, inc=1, device_id=to, device_id_type=MESH)
    pl.semaphore_wait(barrier, planes + 1)

    last = k_ref.shape[0] - WINDOW
    after = {"seq": jnp.minimum(z + 1, planes - 1), "head": head}
    halo = [
        remote(k_ref.at[pl.ds(last, WINDOW)], tail_k, halo_send.at[0], halo_recv.at[0], after),
        remote(v_ref.at[pl.ds(last, WINDOW)], tail_v, halo_send.at[1], halo_recv.at[1], after),
    ]

    @pl.when(z < planes - 1)
    def _():
        for copy in halo:
            copy.start()

    @pl.when(z == 0)
    def _():
        tail_k[...] = jnp.zeros_like(tail_k)
        tail_v[...] = jnp.zeros_like(tail_v)

    @pl.when(z > 0)
    def _():
        for copy in halo:
            copy.wait_recv()

    lane = lax.broadcasted_iota(jnp.int32, (1, LANES), 1)
    low = lane < HEAD_DIM
    for own, tail, to in ((k_ref, tail_k, kk), (v_ref, tail_v, vv)):
        ext[0:WINDOW] = tail[...].astype(F32)
        ext[WINDOW:] = own[...].astype(F32)
        plain = ext[...]
        turned = pltpu.roll(plain, HEAD_DIM, 1)
        to[0, 0] = jnp.where(low, plain, 0.0).astype(BF16)
        to[0, 1] = jnp.where(low, 0.0, turned).astype(BF16)
        to[1, 0] = jnp.where(low, turned, 0.0).astype(BF16)
        to[1, 1] = jnp.where(low, 0.0, plain).astype(BF16)

    span = 2 * WINDOW
    start = z * k_ref.shape[0]
    heads = q_ref.shape[1] // HEAD_DIM
    pairs_of_group = heads // 4

    def attend(block):
        first = pl.multiple_of(start + block * WINDOW, WINDOW)
        row0 = pl.multiple_of(block * WINDOW, WINDOW)
        prior = pl.multiple_of(jnp.maximum(first - WINDOW, 0), WINDOW)
        seg_own = seg_ref[:, pl.ds(first, WINDOW)]
        seg_prior = seg_ref[:, pl.ds(prior, WINDOW)]
        seg_q = as_column(seg_own)
        i = lax.broadcasted_iota(jnp.int32, (WINDOW, WINDOW), 0)
        j = lax.broadcasted_iota(jnp.int32, (WINDOW, WINDOW), 1)
        sees_prior = (j > i) & (seg_prior.astype(F32) == seg_q) & (first > 0)
        sees_own = (j <= i) & (seg_own.astype(F32) == seg_q)

        for group in range(2):
            keys = jnp.concatenate(
                [kk[group, 0, pl.ds(row0, span)], kk[group, 1, pl.ds(row0, span)]], 0
            )
            values = jnp.concatenate(
                [vv[group, 0, pl.ds(row0, span)], vv[group, 1, pl.ds(row0, span)]], 0
            )

            def pair(at, _):
                number = group * pairs_of_group + at
                columns = pl.ds(pl.multiple_of(number * LANES, LANES), LANES)
                scores = lax.dot_general(
                    q_ref[pl.ds(row0, WINDOW), columns], keys, (((1,), (1,)), ((), ())),
                    preferred_element_type=F32,
                ) * HEAD_DIM ** (-0.5)
                probs = []
                for side in range(2):
                    sink = sink_ref[number * 2 + side]
                    far = jnp.where(sees_prior, scores[:, side * span : side * span + WINDOW], -1e30)
                    near = jnp.where(
                        sees_own, scores[:, side * span + WINDOW : (side + 1) * span], -1e30
                    )
                    top = jnp.maximum(jnp.max(jnp.maximum(far, near), 1, keepdims=True), sink)
                    far, near = jnp.exp(far - top), jnp.exp(near - top)
                    total = jnp.sum(far + near, 1, keepdims=True) + jnp.exp(sink - top)
                    scale = 1.0 / total
                    probs += [(far * scale).astype(BF16), (near * scale).astype(BF16)]
                attended[pl.ds(row0, WINDOW), columns] = jnp.dot(
                    jnp.concatenate(probs, 1), values, preferred_element_type=F32
                ).astype(BF16)
                return 0

            lax.fori_loop(0, pairs_of_group, pair, 0)

    mine_core = pl.ds(pl.multiple_of(core * rows, rows), rows)
    its_core = pl.ds(pl.multiple_of((1 - core) * rows, rows), rows)
    tile = 512 if width % 512 == 0 else LANES
    to_core = []
    for turn in range(2):
        block = (1 - x) if turn == 0 else x
        attend(block)
        if turn == 0:
            loads[0].wait()
        row0 = pl.multiple_of(block * WINDOW, WINDOW)

        def project(n, _):
            columns = pl.ds(pl.multiple_of(n * tile, tile), tile)
            proj[turn, :, columns] = jnp.dot(
                attended[pl.ds(row0, WINDOW)], wo[:, columns], preferred_element_type=F32
            ).astype(BF16)
            return 0

        lax.fori_loop(0, width // tile, project, 0)
        copy = remote(
            proj.at[turn, its_core], proj_core.at[turn], pc_send.at[turn], pc_recv.at[turn], other_core
        )
        copy.start()
        to_core.append(copy)
        if turn == 0:
            copy.wait_recv()
            proj_x[...] = (
                proj[0, mine_core].astype(F32) + proj_core[0].astype(F32)
            ).astype(BF16)
            over_x = remote(proj_x, proj_got, px_send.at[0], px_recv.at[0], other_x)
            over_x.start()

    lanes = lax.broadcasted_iota(jnp.int32, (rows, LANES), 1)
    weight = jnp.zeros((rows, LANES), F32)
    for choice in range(ids_ref.shape[1]):
        named = ids_ref[:, choice : choice + 1]
        hit = (lanes == named) | (lanes == named + experts) | (lanes == named + 2 * experts)
        weight += jnp.where(hit, rw_ref[:, choice : choice + 1], 0.0)
    first_term = weight.astype(BF16).astype(F32)
    second_term = (weight - first_term).astype(BF16).astype(F32)
    third_term = weight - first_term - second_term
    term = jnp.where(
        lanes < experts, first_term, jnp.where(lanes < 2 * experts, second_term, third_term)
    )

    mine = pl.ds(pl.multiple_of((core * 2 + x) * rows, rows), rows)
    its_x = pl.ds(pl.multiple_of((core * 2 + 1 - x) * rows, rows), rows)
    both_mine = pl.ds(pl.multiple_of(core * 2 * rows, rows), 2 * rows)
    both_other = pl.ds(pl.multiple_of((1 - core) * 2 * rows, rows), 2 * rows)

    to_core[1].wait_recv()
    over_x.wait_recv()
    state = (
        res_ref[...].astype(F32)
        + proj[1, mine_core].astype(F32)
        + proj_core[1].astype(F32)
        + proj_got[...].astype(F32)
    )
    hidden[...] = state
    variance = jnp.mean(state * state, -1, keepdims=True)
    xbuf[z, mine, 0:width] = (state * lax.rsqrt(variance + 1e-05) * gain_ref[...]).astype(BF16)
    xbuf[z, mine, width:] = term.astype(BF16)

    orders = [
        sorted(range(planes), key=lambda p, own=own: (abs(p - own), p)) for own in range(planes)
    ]
    order = [pick([orders[own][step] for own in range(planes)], z) for step in range(planes)]

    def gather_z(step):
        there = order[step]
        part = xbuf.at[z, mine]
        return remote(part, part, gz_send.at[step], gz_recv.at[z], {"seq": there, "head": head})

    def gather_z_got(step):
        part = xbuf.at[order[step], mine]
        return remote(part, part, gz_send.at[step], gz_recv.at[order[step]], {"seq": order[step], "head": head})

    def gather_x(step):
        part = xbuf.at[order[step], mine]
        return remote(part, part, gx_send.at[order[step]], gx_recv.at[order[step]], other_x)

    def gather_x_got(step):
        part = xbuf.at[order[step], its_x]
        return remote(part, part, gx_send.at[order[step]], gx_recv.at[order[step]], other_x)

    def gather_core(step):
        part = xbuf.at[order[step], both_mine]
        return remote(part, part, gc_send.at[order[step]], gc_recv.at[order[step]], other_core)

    def gather_core_got(step):
        part = xbuf.at[order[step], both_other]
        return remote(part, part, gc_send.at[order[step]], gc_recv.at[order[step]], other_core)

    def sum_core(step):
        p = order[step]
        return remote(obuf.at[p, both_other], rc.at[p], rc_send.at[p], rc_recv.at[p], other_core)

    def sum_x(step):
        p = order[step]
        return remote(s_out.at[p], rx.at[p], rx_send.at[p], rx_recv.at[p], other_x)

    def sum_z(step):
        p = order[step]
        return remote(s_own.at[p], rz.at[z], rz_send.at[p], rz_recv.at[z], {"seq": p, "head": head})

    def sum_z_got(step):
        p = order[step]
        return remote(s_own.at[p], rz.at[p], rz_send.at[p], rz_recv.at[p], {"seq": p, "head": head})

    its_x_part = pl.ds(pl.multiple_of((1 - x) * rows, rows), rows)
    my_x_part = pl.ds(pl.multiple_of(x * rows, rows), rows)
    at_core = pl.multiple_of(core * 2 * rows, rows)

    def after_core(step):
        p = order[step]
        sum_core(step).wait_recv()
        s_out[p] = (
            obuf[p, pl.ds(pl.multiple_of(at_core + (1 - x) * rows, rows), rows)].astype(F32)
            + rc[p, its_x_part].astype(F32)
        ).astype(BF16)
        sum_x(step).start()

    def after_x(step):
        p = order[step]
        sum_x(step).wait_recv()
        total = (
            obuf[p, pl.ds(pl.multiple_of(at_core + x * rows, rows), rows)].astype(F32)
            + rc[p, my_x_part].astype(F32)
            + rx[p].astype(F32)
        )
        if step == 0:
            hidden[...] += total
        else:
            s_own[p] = total.astype(BF16)
            sum_z(step).start()

    gather_x(0).start()
    for step in range(1, planes):
        gather_z(step).start()
    gather_x_got(0).wait_recv()
    gather_core(0).start()
    for load in loads[1:]:
        load.wait()
    expert = (z * 4 + head) // 2
    piece = 256 if ff % 256 == 0 else LANES

    for step in range(planes):
        p = order[step]
        if step + 1 < planes:
            gather_z_got(step + 1).wait_recv()
            gather_x(step + 1).start()
        gather_core_got(step).wait_recv()

        def hidden_units(n, _):
            columns = pl.ds(pl.multiple_of(n * piece, piece), piece)
            normed = xbuf[p, :, 0:width]
            g = jnp.minimum(jnp.dot(normed, gate[:, columns], preferred_element_type=F32), 7.0)
            u = jnp.clip(jnp.dot(normed, up[:, columns], preferred_element_type=F32), -7.0, 7.0)
            act[:, columns] = ((u + 1.0) * g * jax.nn.sigmoid(1.702 * g)).astype(BF16)
            return 0

        lax.fori_loop(0, ff // piece, hidden_units, 0)
        if step >= 1:
            after_core(step - 1)
        if step + 1 < planes:
            gather_x_got(step + 1).wait_recv()
            gather_core(step + 1).start()
        terms = xbuf[p, :, width:].astype(F32)
        at = lax.broadcasted_iota(jnp.int32, terms.shape, 1)
        hit = (at == expert) | (at == expert + experts) | (at == expert + 2 * experts)
        share = jnp.sum(jnp.where(hit, terms, 0.0), 1, keepdims=True)

        def outputs(n, _):
            columns = pl.ds(pl.multiple_of(n * tile, tile), tile)
            obuf[p, :, columns] = (
                jnp.dot(act[...], down[:, columns], preferred_element_type=F32) * share
            ).astype(BF16)
            return 0

        lax.fori_loop(0, width // tile, outputs, 0)
        sum_core(step).start()
        if step >= 1:
            after_x(step - 1)
    after_core(planes - 1)
    after_x(planes - 1)
    total = hidden[...]
    for step in range(1, planes):
        sum_z_got(step).wait_recv()
        total += rz[order[step]].astype(F32)
    out_ref[...] = total.astype(BF16)

    @pl.when(z < planes - 1)
    def _():
        for copy in halo:
            copy.wait_send()

    for copy in to_core + [over_x]:
        copy.wait_send()
    for step in range(planes):
        gather_x(step).wait_send()
        gather_core(step).wait_send()
        sum_core(step).wait_send()
        sum_x(step).wait_send()
        if step:
            gather_z(step).wait_send()
            sum_z(step).wait_send()


def fused(
    planes, query_states, key_states, value_states, sink_logits, segment_ids, residual, out_weight,
    norm_gain, expert_ids, route_weights, gate_proj, up_proj, down_proj,
):
    rows, width = residual.shape
    ff = gate_proj.shape[2]
    plane = 4 * rows
    tokens = query_states.shape[0]
    vmem, hbm = pl.BlockSpec(memory_space=pltpu.VMEM), pl.BlockSpec(memory_space=pl.ANY)
    smem = pl.BlockSpec(memory_space=pltpu.SMEM)
    dma = pltpu.SemaphoreType.DMA
    return pl.pallas_call(
        functools.partial(layer_kernel, planes, gate_proj.shape[0] * planes * 4 // 2),
        out_shape=jax.ShapeDtypeStruct((rows, width), BF16),
        in_specs=[vmem, vmem, vmem, smem, vmem, vmem, hbm, vmem, vmem, vmem, hbm, hbm, hbm],
        out_specs=vmem,
        scratch_shapes=[
            pltpu.VMEM(out_weight.shape, BF16),
            pltpu.VMEM(gate_proj.shape[1:], BF16),
            pltpu.VMEM(up_proj.shape[1:], BF16),
            pltpu.VMEM(down_proj.shape[1:], BF16),
            pltpu.VMEM((WINDOW, LANES), BF16),
            pltpu.VMEM((WINDOW, LANES), BF16),
            pltpu.VMEM((tokens + WINDOW, LANES), F32),
            pltpu.VMEM((2, 2, tokens + WINDOW, LANES), BF16),
            pltpu.VMEM((2, 2, tokens + WINDOW, LANES), BF16),
            pltpu.VMEM(query_states.shape, BF16),
            pltpu.VMEM((2, WINDOW, width), BF16),
            pltpu.VMEM((2, rows, width), BF16),
            pltpu.VMEM((rows, width), BF16),
            pltpu.VMEM((rows, width), BF16),
            pltpu.VMEM((rows, width), F32),
            pltpu.VMEM((planes, plane, width + LANES), BF16),
            pltpu.VMEM((plane, ff), BF16),
            pltpu.VMEM((planes, plane, width), BF16),
            pltpu.VMEM((planes, plane // 2, width), BF16),
            pltpu.VMEM((planes, rows, width), BF16),
            pltpu.VMEM((planes, rows, width), BF16),
            pltpu.VMEM((planes, rows, width), BF16),
            pltpu.VMEM((planes, rows, width), BF16),
            dma((4,)),
            *[dma((2,))] * 4,
            *[dma((1,))] * 2,
            *[dma((planes,))] * 12,
        ],
        compiler_params=pltpu.CompilerParams(
            collective_id=0, has_side_effects=True, vmem_limit_bytes=52 << 20
        ),
    )(
        query_states, key_states, value_states, sink_logits, segment_ids.reshape(1, -1), residual,
        out_weight, norm_gain.reshape(1, -1), expert_ids, route_weights, gate_proj, up_proj, down_proj,
    )


def choose(mesh, *arrays):
    query_states, key_states, residual, expert_ids = arrays[0], arrays[1], arrays[5], arrays[8]
    planes, heads, pair = mesh.shape["seq"], mesh.shape["head"], mesh.shape["pair"]
    rows = residual.shape[0]
    experts = planes * heads // 2
    sources = planes * heads * pair
    capacity = min(rows, max(2, 3 * rows * expert_ids.shape[1] // (2 * experts)))
    suits = (
        pair == 1
        and heads == 4
        and planes > 1
        and 3 * experts <= LANES
        and key_states.shape[1] == 2 * HEAD_DIM
        and 2 * HEAD_DIM == LANES
        and query_states.shape[0] == 2 * WINDOW
        and rows * 4 == query_states.shape[0]
        and sources * rows <= 2 * sources * capacity
    )
    if suits:
        return fused(planes, *arrays)
    return per_device(*arrays)


def solution(mesh):
    in_specs = (
        P(("group", "seq"), ("head", "pair")),
        P(("group", "seq"), "head"),
        P(("group", "seq"), "head"),
        P(("head", "pair")),
        P("group"),
        P(("group", "seq", "head", "pair"), None),
        P(("head", "pair"), None),
        P(),
        P(("group", "seq", "head", "pair"), None),
        P(("group", "seq", "head", "pair"), None),
        P(("seq", "head"), None, "pair"),
        P(("seq", "head"), None, "pair"),
        P(("seq", "head"), "pair", None),
    )
    out_specs = P(("group", "seq", "head", "pair"), None)
    return jax.shard_map(
        functools.partial(choose, mesh), mesh=mesh, in_specs=in_specs, out_specs=out_specs, check_vma=False
    )
```

```python
import functools

import jax
import jax.numpy as jnp
from jax import lax
from jax.experimental import pallas as pl
from jax.experimental.pallas import tpu as pltpu
from jax.sharding import PartitionSpec as P

HEADS = 64
KV_HEADS = 8
HEAD_DIM = 64
WINDOW = 128


def passed_along(value, axis, by):
    peers = lax.axis_size(axis)
    pairs = [(i, i + by) for i in range(peers) if 0 <= i + by < peers]
    return lax.ppermute(value, axis, pairs)


def partner(value, axis, distance):
    return lax.ppermute(value, axis, [(i, i ^ 1 << distance) for i in range(lax.axis_size(axis))])


def round_keep(values):
    return lax.optimization_barrier(values.astype(jnp.bfloat16)).astype(jnp.float32)


def window_attention(
    query_block, key_block, value_block, query_pos, key_pos, query_seg, key_seg, sink_logits
):
    scores = jnp.einsum(
        "qhd,khd->hqk", query_block, key_block, preferred_element_type=jnp.float32
    ) * HEAD_DIM ** (-0.5)
    visible = (key_pos[None, :] <= query_pos[:, None]) & (
        query_pos[:, None] - key_pos[None, :] < WINDOW
    )
    visible = visible & (key_pos[None, :] >= 0) & (key_seg[None, :] == query_seg[:, None])
    masked = jnp.where(visible[None], scores, -1e30)
    row_max = jnp.maximum(jnp.max(masked, -1), sink_logits[:, None])
    weights_exp = jnp.exp(masked - row_max[..., None])
    denominator = jnp.sum(weights_exp, -1) + jnp.exp(sink_logits[:, None] - row_max)
    probs = (weights_exp / denominator[..., None]).astype(jnp.bfloat16)
    attended = jnp.einsum("hqk,khd->qhd", probs, value_block, preferred_element_type=jnp.float32)
    return attended.astype(jnp.bfloat16)


def per_device(
    query_states,
    key_states,
    value_states,
    sink_logits,
    segment_ids,
    residual,
    out_weight,
    norm_gain,
    expert_ids,
    route_weights,
    gate_proj,
    up_proj,
    down_proj,
):
    tok_rows = query_states.shape[0]
    local_heads = query_states.shape[1] // HEAD_DIM
    local_groups = key_states.shape[1] // HEAD_DIM
    group_size = HEADS // KV_HEADS
    tail_keys, tail_values = passed_along(
        (key_states[tok_rows - WINDOW :], value_states[tok_rows - WINDOW :]), "seq", 1
    )
    ext_keys = jnp.concatenate([tail_keys, key_states], 0).reshape(
        tok_rows + WINDOW, local_groups, HEAD_DIM
    )
    ext_values = jnp.concatenate([tail_values, value_states], 0).reshape(
        tok_rows + WINDOW, local_groups, HEAD_DIM
    )
    kv_owner = (
        lax.axis_index("pair") * local_heads + jnp.arange(local_heads, dtype=jnp.int32)
    ) // group_size
    head_select = (kv_owner[:, None] == jnp.arange(local_groups, dtype=jnp.int32)[None, :]).astype(
        jnp.bfloat16
    )
    keys_per_head = jnp.einsum(
        "kcd,hc->khd", ext_keys, head_select, preferred_element_type=jnp.float32
    ).astype(jnp.bfloat16)
    values_per_head = jnp.einsum(
        "kcd,hc->khd", ext_values, head_select, preferred_element_type=jnp.float32
    ).astype(jnp.bfloat16)
    query_heads = query_states.reshape(tok_rows, local_heads, HEAD_DIM)
    seq_start = lax.axis_index("seq") * tok_rows
    seg_padded = jnp.concatenate([jnp.full((WINDOW,), -1, jnp.int32), segment_ids], 0)
    block_rows = min(512, tok_rows)

    def attend(block_index):
        first_row = block_index * block_rows
        query_pos = seq_start + first_row + jnp.arange(block_rows, dtype=jnp.int32)
        key_pos = seq_start + first_row - WINDOW + jnp.arange(block_rows + WINDOW, dtype=jnp.int32)
        query_seg = lax.dynamic_slice_in_dim(segment_ids, seq_start + first_row, block_rows, 0)
        key_seg = lax.dynamic_slice_in_dim(
            seg_padded, seq_start + first_row, block_rows + WINDOW, 0
        )
        return window_attention(
            query_heads,
            keys_per_head,
            values_per_head,
            query_pos,
            key_pos,
            query_seg,
            key_seg,
            sink_logits,
        )

    attended = lax.map(attend, jnp.arange(tok_rows // block_rows, dtype=jnp.int32))
    attended = attended.reshape(tok_rows, local_heads * HEAD_DIM)
    shard_rows = residual.shape[0]
    width = residual.shape[1]
    projected = lax.psum_scatter(
        round_keep(jnp.dot(attended, out_weight, preferred_element_type=jnp.float32)).astype(
            jnp.bfloat16
        ),
        ("head", "pair"),
        scatter_dimension=0,
        tiled=True,
    ).astype(jnp.float32)
    hidden_state = residual.astype(jnp.float32) + projected
    variance = jnp.mean(hidden_state * hidden_state, -1, keepdims=True)
    normed = (hidden_state * lax.rsqrt(variance + 1e-05) * norm_gain).astype(jnp.bfloat16)
    top_count = expert_ids.shape[1]
    experts = lax.axis_size("seq") * lax.axis_size("head") // 2
    capacity = min(shard_rows, max(2, 3 * shard_rows * top_count // (2 * experts)))
    flat_ids = expert_ids.reshape(-1)
    onehot = (flat_ids[:, None] == jnp.arange(experts, dtype=jnp.int32)[None, :]).astype(jnp.int32)
    places = jnp.arange(flat_ids.shape[0], dtype=jnp.int32)
    earlier = (places[None, :] < places[:, None]).astype(jnp.bfloat16)
    before = jnp.dot(
        earlier, onehot.astype(jnp.bfloat16), preferred_element_type=jnp.float32
    ).astype(jnp.int32)
    slot_rank = jnp.sum(before * onehot, -1)
    slot_index = flat_ids * capacity + slot_rank
    dispatch_mat = (
        slot_index[None, :] == jnp.arange(experts * capacity, dtype=jnp.int32)[:, None]
    ).astype(jnp.bfloat16)
    repeated = jnp.repeat(normed, top_count, axis=0)
    outgoing = jnp.dot(dispatch_mat, repeated, preferred_element_type=jnp.float32).astype(
        jnp.bfloat16
    )
    outgoing = outgoing.reshape(experts, capacity, width)
    half_idx = lax.axis_index("head") % 2
    half_width = width // 2
    split_rows = outgoing.reshape(experts, capacity, 2, half_width).transpose(0, 2, 1, 3)
    split_rows = split_rows.reshape(2 * experts, capacity, half_width)
    own_half = lax.all_to_all(split_rows, ("seq", "head"), split_axis=0, concat_axis=0, tiled=True)
    other_half = partner(own_half, "head", 0)
    arrived = jnp.where(
        half_idx == 0,
        jnp.concatenate([own_half, other_half], -1),
        jnp.concatenate([other_half, own_half], -1),
    )
    gate_local = gate_proj[0]
    up_local = up_proj[0]
    down_local = down_proj[0]
    piece_rows = lax.all_gather(arrived, "pair", axis=0, tiled=True)
    flat_rows = piece_rows.reshape(-1, width)
    gate_val = jnp.minimum(jnp.dot(flat_rows, gate_local, preferred_element_type=jnp.float32), 7.0)
    up_val = jnp.clip(jnp.dot(flat_rows, up_local, preferred_element_type=jnp.float32), -7.0, 7.0)
    activated = ((up_val + 1.0) * gate_val * jax.nn.sigmoid(1.702 * gate_val)).astype(jnp.bfloat16)
    partial_value = round_keep(jnp.dot(activated, down_local, preferred_element_type=jnp.float32))
    quarter_terms = partial_value.reshape(piece_rows.shape)
    pair_sums = lax.psum_scatter(
        quarter_terms.astype(jnp.bfloat16), "pair", scatter_dimension=0, tiled=True
    ).astype(jnp.float32)
    kept_half = lax.dynamic_slice_in_dim(pair_sums, half_idx * half_width, half_width, 2)
    given_half = lax.dynamic_slice_in_dim(pair_sums, (1 - half_idx) * half_width, half_width, 2)
    partner_half = partner(given_half.astype(jnp.bfloat16), "head", 0).astype(given_half.dtype)
    merged = kept_half + partner_half
    returned = lax.all_to_all(
        merged.astype(jnp.bfloat16), ("seq", "head"), split_axis=0, concat_axis=0, tiled=True
    ).astype(merged.dtype)
    expert_out = (
        returned.reshape(experts, 2, capacity, half_width)
        .transpose(0, 2, 1, 3)
        .reshape(experts, capacity, width)
    )
    slot_table = slot_index.reshape(shard_rows, top_count)
    columns_all = jnp.arange(experts * capacity, dtype=jnp.int32)
    combine_mat = jnp.sum(
        jnp.where(
            slot_table[:, :, None] == columns_all[None, None, :], route_weights[:, :, None], 0.0
        ),
        axis=1,
    )
    mixture = jnp.dot(
        combine_mat, expert_out.reshape(experts * capacity, width), precision=lax.Precision.HIGHEST
    )
    return (hidden_state + mixture).astype(jnp.bfloat16)


BF16, F32 = jnp.bfloat16, jnp.float32
MESH = pl.DeviceIdType.MESH
LANES = 128


def pick(table, index):
    result = jnp.int32(table[0])
    for i in range(1, len(table)):
        result = jnp.where(index == i, jnp.int32(table[i]), result)
    return result


def as_column(row, dtype=F32):
    n = row.shape[1]
    at = lax.broadcasted_iota(jnp.int32, (n, n), 0) == lax.broadcasted_iota(jnp.int32, (n, n), 1)
    return jnp.sum(jnp.where(at, row.astype(F32), 0.0), 1, keepdims=True)


def layer_kernel(
    planes, experts, split,
    q_ref, k_ref, v_ref, sink_ref, seg_ref, res_ref, wo_hbm, gain_ref, ids_ref, rw_ref,
    gate_hbm, up_hbm, down_hbm,
    out_ref,
    wo, gate, up, down, tail_k, tail_v, ext, kk, vv, attended, proj, proj_core, proj_x, proj_got,
    hidden, xbuf, act, obuf, rc, s_out, rx, s_own, rz,
    w_sem, halo_send, halo_recv, pc_send, pc_recv, px_send, px_recv,
    gz_send, gz_recv, gx_send, gx_recv, gc_send, gc_recv,
    rc_send, rc_recv, rx_send, rx_recv, rz_send, rz_recv,
):
    z, head = lax.axis_index("seq"), lax.axis_index("head")
    x, core = head // 2, head % 2
    other_core = {"seq": z, "head": x * 2 + 1 - core}
    other_x = {"seq": z, "head": (1 - x) * 2 + core}
    rows, width = res_ref.shape
    ff = gate.shape[1]

    def remote(src, dst, send, recv, to):
        return pltpu.make_async_remote_copy(
            src_ref=src, dst_ref=dst, send_sem=send, recv_sem=recv, device_id=to, device_id_type=MESH
        )

    loads = [
        pltpu.make_async_copy(wo_hbm, wo, w_sem.at[0]),
        pltpu.make_async_copy(gate_hbm.at[0], gate, w_sem.at[1]),
        pltpu.make_async_copy(up_hbm.at[0], up, w_sem.at[2]),
        pltpu.make_async_copy(down_hbm.at[0], down, w_sem.at[3]),
    ]
    for load in loads:
        load.start()

    barrier = pltpu.get_barrier_semaphore()
    pl.semaphore_signal(barrier, inc=1, device_id=other_core, device_id_type=MESH)
    pl.semaphore_signal(barrier, inc=1, device_id=other_x, device_id_type=MESH)
    for far in range(1, planes):
        to = {"seq": lax.rem(z + far, planes), "head": head}
        pl.semaphore_signal(barrier, inc=1, device_id=to, device_id_type=MESH)
    pl.semaphore_wait(barrier, planes + 1)

    last = k_ref.shape[0] - WINDOW
    after = {"seq": jnp.minimum(z + 1, planes - 1), "head": head}
    halo = [
        remote(k_ref.at[pl.ds(last, WINDOW)], tail_k, halo_send.at[0], halo_recv.at[0], after),
        remote(v_ref.at[pl.ds(last, WINDOW)], tail_v, halo_send.at[1], halo_recv.at[1], after),
    ]

    @pl.when(z < planes - 1)
    def _():
        for copy in halo:
            copy.start()

    @pl.when(z == 0)
    def _():
        tail_k[...] = jnp.zeros_like(tail_k)
        tail_v[...] = jnp.zeros_like(tail_v)

    @pl.when(z > 0)
    def _():
        for copy in halo:
            copy.wait_recv()

    lane = lax.broadcasted_iota(jnp.int32, (1, LANES), 1)
    low = lane < HEAD_DIM
    for own, tail, to in ((k_ref, tail_k, kk), (v_ref, tail_v, vv)):
        ext[0:WINDOW] = tail[...].astype(F32)
        ext[WINDOW:] = own[...].astype(F32)
        plain = ext[...]
        turned = pltpu.roll(plain, HEAD_DIM, 1)
        to[0, 0] = jnp.where(low, plain, 0.0).astype(BF16)
        to[0, 1] = jnp.where(low, 0.0, turned).astype(BF16)
        to[1, 0] = jnp.where(low, turned, 0.0).astype(BF16)
        to[1, 1] = jnp.where(low, 0.0, plain).astype(BF16)

    span = 2 * WINDOW
    start = z * k_ref.shape[0]
    heads = q_ref.shape[1] // HEAD_DIM
    pairs_of_group = heads // 4

    def attend(block):
        first = pl.multiple_of(start + block * WINDOW, WINDOW)
        row0 = pl.multiple_of(block * WINDOW, WINDOW)
        prior = pl.multiple_of(jnp.maximum(first - WINDOW, 0), WINDOW)
        seg_own = seg_ref[:, pl.ds(first, WINDOW)]
        seg_prior = seg_ref[:, pl.ds(prior, WINDOW)]
        seg_q = as_column(seg_own)
        i = lax.broadcasted_iota(jnp.int32, (WINDOW, WINDOW), 0)
        j = lax.broadcasted_iota(jnp.int32, (WINDOW, WINDOW), 1)
        sees_prior = (j > i) & (seg_prior.astype(F32) == seg_q) & (first > 0)
        sees_own = (j <= i) & (seg_own.astype(F32) == seg_q)

        for group in range(2):
            keys = jnp.concatenate(
                [kk[group, 0, pl.ds(row0, span)], kk[group, 1, pl.ds(row0, span)]], 0
            )
            values = jnp.concatenate(
                [vv[group, 0, pl.ds(row0, span)], vv[group, 1, pl.ds(row0, span)]], 0
            )

            def pair(at, _):
                number = group * pairs_of_group + at
                columns = pl.ds(pl.multiple_of(number * LANES, LANES), LANES)
                scores = lax.dot_general(
                    q_ref[pl.ds(row0, WINDOW), columns], keys, (((1,), (1,)), ((), ())),
                    preferred_element_type=F32,
                ) * HEAD_DIM ** (-0.5)
                probs = []
                for side in range(2):
                    sink = sink_ref[number * 2 + side]
                    far = jnp.where(sees_prior, scores[:, side * span : side * span + WINDOW], -1e30)
                    near = jnp.where(
                        sees_own, scores[:, side * span + WINDOW : (side + 1) * span], -1e30
                    )
                    top = jnp.maximum(jnp.max(jnp.maximum(far, near), 1, keepdims=True), sink)
                    far, near = jnp.exp(far - top), jnp.exp(near - top)
                    total = jnp.sum(far + near, 1, keepdims=True) + jnp.exp(sink - top)
                    scale = 1.0 / total
                    probs += [(far * scale).astype(BF16), (near * scale).astype(BF16)]
                attended[pl.ds(row0, WINDOW), columns] = jnp.dot(
                    jnp.concatenate(probs, 1), values, preferred_element_type=F32
                ).astype(BF16)
                return 0

            lax.fori_loop(0, pairs_of_group, pair, 0)

    mine_core = pl.ds(pl.multiple_of(core * rows, rows), rows)
    its_core = pl.ds(pl.multiple_of((1 - core) * rows, rows), rows)
    tile = 512 if width % 512 == 0 else LANES
    to_core = []
    for turn in range(2):
        block = (1 - x) if turn == 0 else x
        attend(block)
        if turn == 0:
            loads[0].wait()
        row0 = pl.multiple_of(block * WINDOW, WINDOW)

        def project(n, _):
            columns = pl.ds(pl.multiple_of(n * tile, tile), tile)
            proj[turn, :, columns] = jnp.dot(
                attended[pl.ds(row0, WINDOW)], wo[:, columns], preferred_element_type=F32
            ).astype(BF16)
            return 0

        lax.fori_loop(0, width // tile, project, 0)
        copy = remote(
            proj.at[turn, its_core], proj_core.at[turn], pc_send.at[turn], pc_recv.at[turn], other_core
        )
        copy.start()
        to_core.append(copy)
        if turn == 0:
            copy.wait_recv()
            proj_x[...] = (
                proj[0, mine_core].astype(F32) + proj_core[0].astype(F32)
            ).astype(BF16)
            over_x = remote(proj_x, proj_got, px_send.at[0], px_recv.at[0], other_x)
            over_x.start()

    lanes = lax.broadcasted_iota(jnp.int32, (rows, LANES), 1)
    weight = jnp.zeros((rows, LANES), F32)
    for choice in range(ids_ref.shape[1]):
        named = ids_ref[:, choice : choice + 1]
        hit = (lanes == named) | (lanes == named + experts) | (lanes == named + 2 * experts)
        weight += jnp.where(hit, rw_ref[:, choice : choice + 1], 0.0)
    first_term = weight.astype(BF16).astype(F32)
    second_term = (weight - first_term).astype(BF16).astype(F32)
    third_term = weight - first_term - second_term
    term = jnp.where(
        lanes < experts, first_term, jnp.where(lanes < 2 * experts, second_term, third_term)
    )

    mine = pl.ds(pl.multiple_of((core * 2 + x) * rows, rows), rows)
    its_x = pl.ds(pl.multiple_of((core * 2 + 1 - x) * rows, rows), rows)
    both_mine = pl.ds(pl.multiple_of(core * 2 * rows, rows), 2 * rows)
    both_other = pl.ds(pl.multiple_of((1 - core) * 2 * rows, rows), 2 * rows)

    to_core[1].wait_recv()
    over_x.wait_recv()
    state = (
        res_ref[...].astype(F32)
        + proj[1, mine_core].astype(F32)
        + proj_core[1].astype(F32)
        + proj_got[...].astype(F32)
    )
    hidden[...] = state
    variance = jnp.mean(state * state, -1, keepdims=True)
    xbuf[z, mine, 0:width] = (state * lax.rsqrt(variance + 1e-05) * gain_ref[...]).astype(BF16)
    xbuf[z, mine, width:] = term.astype(BF16)

    orders = [
        sorted(range(planes), key=lambda p, own=own: (abs(p - own), p)) for own in range(planes)
    ]
    order = [pick([orders[own][step] for own in range(planes)], z) for step in range(planes)]

    early, late = pl.ds(0, split), pl.ds(split, width + LANES - split)
    parts = (0, 1) if split else (1,)

    def along_z(p, toward, part):
        block = xbuf.at[p, both_mine, early] if part == 0 else xbuf.at[p, mine, late]
        beside = jnp.minimum(z + 1, planes - 1) if toward else jnp.maximum(z - 1, 0)
        return remote(
            block, block, gz_send.at[part, toward, p], gz_recv.at[part, p], {"seq": beside, "head": head}
        )

    def passing(step, act_on):
        p = order[step]

        @pl.when((p <= z) & (z < planes - 1))
        def _():
            act_on(p, 1)

        @pl.when((p >= z) & (z > 0))
        def _():
            act_on(p, 0)

    def arrived(step, part):
        along_z(order[step], 0, part).wait_recv()

    def gather_x(step):
        p = order[step]
        part = xbuf.at[p, mine] if step == 0 else xbuf.at[p, mine, late]
        return remote(part, part, gx_send.at[p], gx_recv.at[p], other_x)

    def gather_x_got(step):
        p = order[step]
        part = xbuf.at[p, its_x] if step == 0 else xbuf.at[p, its_x, late]
        return remote(part, part, gx_send.at[p], gx_recv.at[p], other_x)

    def gather_core(step):
        part = xbuf.at[order[step], both_mine]
        return remote(part, part, gc_send.at[order[step]], gc_recv.at[order[step]], other_core)

    def gather_core_got(step):
        part = xbuf.at[order[step], both_other]
        return remote(part, part, gc_send.at[order[step]], gc_recv.at[order[step]], other_core)

    def sum_core(step):
        p = order[step]
        return remote(obuf.at[p, both_other], rc.at[p], rc_send.at[p], rc_recv.at[p], other_core)

    def sum_x(step):
        p = order[step]
        return remote(s_out.at[p], rx.at[p], rx_send.at[p], rx_recv.at[p], other_x)

    def sum_z(step):
        p = order[step]
        return remote(s_own.at[p], rz.at[z], rz_send.at[p], rz_recv.at[z], {"seq": p, "head": head})

    def sum_z_got(step):
        p = order[step]
        return remote(s_own.at[p], rz.at[p], rz_send.at[p], rz_recv.at[p], {"seq": p, "head": head})

    its_x_part = pl.ds(pl.multiple_of((1 - x) * rows, rows), rows)
    my_x_part = pl.ds(pl.multiple_of(x * rows, rows), rows)
    at_core = pl.multiple_of(core * 2 * rows, rows)

    def after_core(step):
        p = order[step]
        sum_core(step).wait_recv()
        s_out[p] = (
            obuf[p, pl.ds(pl.multiple_of(at_core + (1 - x) * rows, rows), rows)].astype(F32)
            + rc[p, its_x_part].astype(F32)
        ).astype(BF16)
        sum_x(step).start()

    def after_x(step):
        p = order[step]
        sum_x(step).wait_recv()
        total = (
            obuf[p, pl.ds(pl.multiple_of(at_core + x * rows, rows), rows)].astype(F32)
            + rc[p, my_x_part].astype(F32)
            + rx[p].astype(F32)
        )
        if step == 0:
            hidden[...] += total
        else:
            s_own[p] = total.astype(BF16)
            sum_z(step).start()

    gather_x(0).start()
    passing(0, lambda p, toward: along_z(p, toward, 1).start())
    gather_x_got(0).wait_recv()
    if split:
        passing(0, lambda p, toward: along_z(p, toward, 0).start())
    gather_core(0).start()
    for load in loads[1:]:
        load.wait()
    expert = (z * 4 + head) // 2
    piece = 256 if ff % 256 == 0 else LANES

    for step in range(planes):
        p = order[step]
        if step + 1 < planes:
            arrived(step + 1, 1)
            gather_x(step + 1).start()
            passing(step + 1, lambda p, toward: along_z(p, toward, 1).start())
            if split:
                arrived(step + 1, 0)
                passing(step + 1, lambda p, toward: along_z(p, toward, 0).start())
        gather_core_got(step).wait_recv()

        def hidden_units(n, _):
            columns = pl.ds(pl.multiple_of(n * piece, piece), piece)
            normed = xbuf[p, :, 0:width]
            g = jnp.minimum(jnp.dot(normed, gate[:, columns], preferred_element_type=F32), 7.0)
            u = jnp.clip(jnp.dot(normed, up[:, columns], preferred_element_type=F32), -7.0, 7.0)
            act[:, columns] = ((u + 1.0) * g * jax.nn.sigmoid(1.702 * g)).astype(BF16)
            return 0

        lax.fori_loop(0, ff // piece, hidden_units, 0)
        if step >= 2:
            after_core(step - 1)
        if step + 1 < planes:
            gather_x_got(step + 1).wait_recv()
            gather_core(step + 1).start()
        terms = xbuf[p, :, width:].astype(F32)
        at = lax.broadcasted_iota(jnp.int32, terms.shape, 1)
        hit = (at == expert) | (at == expert + experts) | (at == expert + 2 * experts)
        share = jnp.sum(jnp.where(hit, terms, 0.0), 1, keepdims=True)

        def outputs(n, _):
            columns = pl.ds(pl.multiple_of(n * tile, tile), tile)
            obuf[p, :, columns] = (
                jnp.dot(act[...], down[:, columns], preferred_element_type=F32) * share
            ).astype(BF16)
            return 0

        lax.fori_loop(0, width // tile, outputs, 0)
        sum_core(step).start()
        if step >= 3:
            after_x(step - 2)
    after_core(planes - 1)
    for step in range(max(1, planes - 2), planes - 1):
        after_x(step)
    after_core(0)
    after_x(planes - 1)
    after_x(0)
    total = hidden[...]
    for step in range(1, planes):
        sum_z_got(step).wait_recv()
        total += rz[order[step]].astype(F32)
    out_ref[...] = total.astype(BF16)

    @pl.when(z < planes - 1)
    def _():
        for copy in halo:
            copy.wait_send()

    for copy in to_core + [over_x]:
        copy.wait_send()
    for step in range(planes):
        gather_x(step).wait_send()
        gather_core(step).wait_send()
        sum_core(step).wait_send()
        sum_x(step).wait_send()
        if step:
            sum_z(step).wait_send()
        for part in parts:
            passing(step, lambda p, toward, part=part: along_z(p, toward, part).wait_send())


def fused(
    planes, query_states, key_states, value_states, sink_logits, segment_ids, residual, out_weight,
    norm_gain, expert_ids, route_weights, gate_proj, up_proj, down_proj,
):
    rows, width = residual.shape
    ff = gate_proj.shape[2]
    plane = 4 * rows
    tokens = query_states.shape[0]
    split = (width + LANES) // 6 // LANES * LANES
    vmem, hbm = pl.BlockSpec(memory_space=pltpu.VMEM), pl.BlockSpec(memory_space=pl.ANY)
    smem = pl.BlockSpec(memory_space=pltpu.SMEM)
    dma = pltpu.SemaphoreType.DMA
    return pl.pallas_call(
        functools.partial(layer_kernel, planes, gate_proj.shape[0] * planes * 4 // 2, split),
        out_shape=jax.ShapeDtypeStruct((rows, width), BF16),
        in_specs=[vmem, vmem, vmem, smem, vmem, vmem, hbm, vmem, vmem, vmem, hbm, hbm, hbm],
        out_specs=vmem,
        scratch_shapes=[
            pltpu.VMEM(out_weight.shape, BF16),
            pltpu.VMEM(gate_proj.shape[1:], BF16),
            pltpu.VMEM(up_proj.shape[1:], BF16),
            pltpu.VMEM(down_proj.shape[1:], BF16),
            pltpu.VMEM((WINDOW, LANES), BF16),
            pltpu.VMEM((WINDOW, LANES), BF16),
            pltpu.VMEM((tokens + WINDOW, LANES), F32),
            pltpu.VMEM((2, 2, tokens + WINDOW, LANES), BF16),
            pltpu.VMEM((2, 2, tokens + WINDOW, LANES), BF16),
            pltpu.VMEM(query_states.shape, BF16),
            pltpu.VMEM((2, WINDOW, width), BF16),
            pltpu.VMEM((2, rows, width), BF16),
            pltpu.VMEM((rows, width), BF16),
            pltpu.VMEM((rows, width), BF16),
            pltpu.VMEM((rows, width), F32),
            pltpu.VMEM((planes, plane, width + LANES), BF16),
            pltpu.VMEM((plane, ff), BF16),
            pltpu.VMEM((planes, plane, width), BF16),
            pltpu.VMEM((planes, plane // 2, width), BF16),
            pltpu.VMEM((planes, rows, width), BF16),
            pltpu.VMEM((planes, rows, width), BF16),
            pltpu.VMEM((planes, rows, width), BF16),
            pltpu.VMEM((planes, rows, width), BF16),
            dma((4,)),
            *[dma((2,))] * 4,
            *[dma((1,))] * 2,
            dma((2, 2, planes)),
            dma((2, planes)),
            *[dma((planes,))] * 10,
        ],
        compiler_params=pltpu.CompilerParams(
            collective_id=0, has_side_effects=True, vmem_limit_bytes=52 << 20
        ),
    )(
        query_states, key_states, value_states, sink_logits, segment_ids.reshape(1, -1), residual,
        out_weight, norm_gain.reshape(1, -1), expert_ids, route_weights, gate_proj, up_proj, down_proj,
    )


def choose(mesh, *arrays):
    query_states, key_states, residual, expert_ids = arrays[0], arrays[1], arrays[5], arrays[8]
    planes, heads, pair = mesh.shape["seq"], mesh.shape["head"], mesh.shape["pair"]
    rows = residual.shape[0]
    experts = planes * heads // 2
    sources = planes * heads * pair
    capacity = min(rows, max(2, 3 * rows * expert_ids.shape[1] // (2 * experts)))
    suits = (
        pair == 1
        and heads == 4
        and planes > 1
        and 3 * experts <= LANES
        and key_states.shape[1] == 2 * HEAD_DIM
        and 2 * HEAD_DIM == LANES
        and query_states.shape[0] == 2 * WINDOW
        and rows * 4 == query_states.shape[0]
        and sources * rows <= 2 * sources * capacity
    )
    if suits:
        return fused(planes, *arrays)
    return per_device(*arrays)


def solution(mesh):
    in_specs = (
        P(("group", "seq"), ("head", "pair")),
        P(("group", "seq"), "head"),
        P(("group", "seq"), "head"),
        P(("head", "pair")),
        P("group"),
        P(("group", "seq", "head", "pair"), None),
        P(("head", "pair"), None),
        P(),
        P(("group", "seq", "head", "pair"), None),
        P(("group", "seq", "head", "pair"), None),
        P(("seq", "head"), None, "pair"),
        P(("seq", "head"), None, "pair"),
        P(("seq", "head"), "pair", None),
    )
    out_specs = P(("group", "seq", "head", "pair"), None)
    return jax.shard_map(
        functools.partial(choose, mesh), mesh=mesh, in_specs=in_specs, out_specs=out_specs, check_vma=False
    )
```
